32 devices in a mesh: seq: 8 (over z, y), head: 4 (over x, core).
Axes of the slice: x: 2, y: 2, z: 4, core: 2. Of those that a mesh axis runs over, the one named last changes fastest.
Arguments:
- queries: bfloat16 [4096, 4096], P('seq', 'head'), may hold values from -4 to 4
- key_vectors: bfloat16 [4096, 4096], P('seq', 'head'), may hold values from -6 to 6
- output_grad: bfloat16 [4096, 4096], P('seq', 'head'), may hold values from -6 to 6
- value_weight: bfloat16 [6144, 4096], P('seq', 'head'), may hold values from -0.078125 to 0.078125
- decay_rate: float32 [32], P('head'), may hold values from 4.8828125e-05 to 0.035
- doc_lengths: int32 [4], replicated, may hold values from 1 to 2048, 4096 in all
- owner_block: int32 [4096, 1], P('seq'), may hold values from 0 to 31; in each aligned block of 128 rows (0 to 127, 128 to 255, ...) at most 8 rows name the same one
- row_offset: int32 [4096], P('seq'), may hold values from 0 to 3127
Outputs:
- row_grads: bfloat16 [32, 32, 8, 6144], P(('seq', 'head'))
The draws below stay inside these ranges and needn't reach their ends.
Inputs may be any that keep to these rules, and one draw needn't show every extreme that they name: `doc_lengths`: the longest document has exactly 2048 positions. `owner_block`: in each aligned block of 128 positions no owner is named more than 8 times; some block names some owner exactly 8 times.
All inputs are finite; a program needn't handle non-finite values.
Results may differ from the reference program's by a relative error of at most 0.0071.
Values may be sent and summed in bfloat16 or wider, within the bound.
A program may use at most 128 MiB of HBM per device.

```python
import math
import jax
import jax.numpy as jnp
import numpy as np
from jax import lax

D = 6144
HEADS = 32
HEAD_DIM = 128
DOCS = 4
TOK_DEV = 512
TOKENS = 4096
ROWS_BLK = 128
VROWS = 3128
CAP = 8
N_HEAD = 4
DEVICES = 32


def draw_decay_rate(key, part):
    key_pick, key_slow, key_fast = jax.random.split(key, 3)
    slow_rate = jnp.exp(jnp.log(0.2 / TOKENS) + jax.random.uniform(key_slow, (HEADS,), jnp.float32) * jnp.log(10.0))
    fast_rate = jnp.exp(jnp.log(0.02) + jax.random.uniform(key_fast, (HEADS,), jnp.float32) * jnp.log(1.75))
    slow_share = 0.5
    slow_pick = jax.random.uniform(key_pick, (HEADS,), jnp.float32) < slow_share
    return jnp.where(slow_pick, slow_rate, fast_rate).astype(jnp.float32)


def touch_ends(entries, stream_key, least, top_value):
    dims = entries.shape
    spot = [jax.random.randint(jax.random.fold_in(stream_key, axis), (), 0, dims[axis]) for axis in range(len(dims))]
    entries = entries.at[tuple(spot)].set(least)
    longest = dims.index(max(dims))
    spot[longest] = (spot[longest] + 1) % dims[longest]
    return entries.at[tuple(spot)].set(top_value)


def block_levels(rng, shape, cuts, least, largest):
    loudness, own = 1.0, jax.random.fold_in(rng, 6)
    for position, shards_of in cuts:
        steps = jnp.exp(jax.random.uniform(jax.random.fold_in(own, position), (shards_of,), jnp.float32, least / len(cuts), largest / len(cuts)))
        loudness = loudness * jnp.repeat(steps, shape[position] // shards_of).reshape([-1 if axis == position else 1 for axis in range(len(shape))])
    return loudness


def split_up(count, total, reach, lean):
    portions = [(1 << 20) // math.isqrt(grade ** lean) + 1 for grade in range(2, count + 1)]
    spare, counts = total - reach - (count - 1), [1] * (count - 1)
    while spare > 0:
        free = [i for i in range(count - 1) if counts[i] < reach]
        pool, budget = sum([portions[i] for i in free]), spare
        for i in free:
            addition = min(reach - counts[i], max(1, budget * portions[i] // pool), spare)
            counts[i] = counts[i] + addition
            spare = spare - addition
    return np.array([reach] + counts)


def ragged(key, count, total, most, lean):
    if count == 2:
        one = jax.random.randint(key, (), max(1, total - most), min(most, total - 1) + 1)
        return jnp.stack([one, total - one])
    tallies = jnp.asarray(split_up(count, total, most, lean), jnp.int32)
    couples = (count - 1) // 2
    donor, sink = tallies[1:1 + 2 * couples:2], tallies[2:2 + 2 * couples:2]
    slack = jnp.minimum(donor - 1, most - sink)
    moved = jax.random.randint(jax.random.fold_in(key, 1), (couples,), 0, 1 << 20) % (slack + 1)
    tallies = tallies.at[1:1 + 2 * couples:2].set(donor - moved).at[2:2 + 2 * couples:2].set(sink + moved)
    return tallies[jax.random.permutation(jax.random.fold_in(key, 2), count)]


def deal_out(own_key, own, number, rows, number_of, top, limit, lean):
    order = jax.random.permutation(own_key, number_of)
    crowded, common = shares(number_of, rows * top, limit, lean, True), shares(number_of, rows * top, limit, lean, False)
    places = jnp.arange(number_of)

    def named(lengths, turn):
        used = int((lengths > 0).sum())
        fixed = max(1, used // 4)
        moved = fixed + (places - fixed + turn * (used - fixed)) % max(1, number_of - fixed)
        return jnp.zeros((number_of,), jnp.int32).at[order[jnp.where(places < fixed, places, moved)]].set(jnp.asarray(lengths, jnp.int32))

    lengths = jnp.where(number % 4 == 0, named(crowded, number // 4), named(common, number - number // 4 - 1))
    mixed = jax.random.permutation(jax.random.fold_in(own, 3), number_of)
    donor, receiver = mixed[0:number_of // 2 * 2:2], mixed[1:number_of // 2 * 2:2]
    room = jnp.minimum(lengths[donor] - 1, limit - lengths[receiver]) // 2
    room = jnp.where((donor == order[0]) | (receiver == order[0]) | (lengths[receiver] == 0), 0, jnp.maximum(room, 0))
    moved = jax.random.randint(jax.random.fold_in(own, 4), (number_of // 2,), 0, 1 << 20) % (room + 1)
    lengths = lengths.at[donor].add(-moved).at[receiver].add(moved)
    members = jnp.searchsorted(jnp.cumsum(lengths), jnp.arange(rows * top), side="right").astype(jnp.int32)
    table = members.reshape(top, rows).T
    table = table[jax.random.permutation(jax.random.fold_in(own, 1), rows)]
    turn = jax.random.randint(jax.random.fold_in(own, 2), (rows, 1), 0, top)
    return jnp.take_along_axis(table, (jnp.arange(top)[None, :] + turn) % top, axis=1)


def shares(number_of, total, bound, skew, full):
    loads = [(1 << 20) // math.isqrt(rank ** skew) + 1 for rank in range(1, number_of + 1)]
    largest = bound if full else min(bound, max(-(-total // number_of), total * loads[0] // sum(loads)))
    least = 1 if total - largest >= number_of - 1 else 0
    counts, surplus = [largest] + [least] * (number_of - 1), total - largest - least * (number_of - 1)
    while surplus > 0:
        free = [i for i in range(1, number_of) if counts[i] < largest] or [i for i in range(1, number_of) if counts[i] < bound]
        whole, left = sum([loads[i] for i in free]), surplus
        for i in free:
            more = min(bound - counts[i], max(1, left * loads[i] // whole), surplus)
            counts[i] = counts[i] + more
            surplus = surplus - more
    return np.array(counts)


def bell_draw(rng, shape, scale, most, pieces=(), held_as=jnp.bfloat16):
    array = jax.random.normal(rng, shape, jnp.float32) * scale
    if len(pieces) > 0:
        array = block_levels(rng, shape, pieces, -0.22, 0.18) * array
    return jnp.clip(array, min=-most, max=most).astype(held_as)


def setup_inputs(seed: int = 0) -> dict:
    seeds = jax.random.split(jax.random.key(seed), 9)
    queries = bell_draw(seeds[0], (TOKENS, HEADS * HEAD_DIM), 0.25, 4.0, ((0, 8), (1, 4)))
    key_vectors = bell_draw(seeds[1], (TOKENS, HEADS * HEAD_DIM), 1.0, 6.0, ((0, 8), (1, 4)))
    output_grad = bell_draw(seeds[2], (TOKENS, HEADS * HEAD_DIM), 1.0, 6.0, ((0, 8), (1, 4)))
    value_weight = bell_draw(seeds[3], (D, HEADS * HEAD_DIM), D ** -0.5, 0.078125, ((0, 8), (1, 4)))
    decay_rate = draw_decay_rate(jax.random.fold_in(seeds[8], 71), 0)
    doc_lengths = ragged(seeds[5], DOCS, TOKENS, TOKENS // 2, 2).astype(jnp.int32)
    owner_block_keys = jax.random.split(jax.random.fold_in(seeds[6], 1), TOKENS // ROWS_BLK)
    owner_block_turns = jax.random.permutation(jax.random.fold_in(seeds[6], 3), TOKENS // ROWS_BLK)
    owner_block = jax.vmap(lambda own, number: deal_out(jax.random.fold_in(seeds[6], 2), own, number, ROWS_BLK, DEVICES, 1, CAP, 2))(owner_block_keys, owner_block_turns).reshape((TOKENS, 1))
    row_offset = touch_ends(jax.random.randint(seeds[7], (TOKENS,), 0, VROWS), jax.random.fold_in(seeds[7], 1), 0, VROWS - 1).astype(jnp.int32)
    return {"queries": queries, "key_vectors": key_vectors, "output_grad": output_grad, "value_weight": value_weight, "decay_rate": decay_rate, "doc_lengths": doc_lengths, "owner_block": owner_block, "row_offset": row_offset}


def doc_of(positions, doc_ends):
    return jnp.sum((positions[:, None] >= doc_ends[None, :]).astype(jnp.int32), axis=1).astype(jnp.int32)


def intra_terms(query_blk, key_blk, grad_blk, decay_rates, doc_blk, pos_blk):
    scores = jnp.einsum("she,the->hst", key_blk.astype(jnp.float32), query_blk.astype(jnp.float32)) / HEAD_DIM
    distance = pos_blk[None, :] - pos_blk[:, None]
    allowed = (distance >= 0) & (doc_blk[:, None] == doc_blk[None, :])
    spans = jnp.maximum(distance, 0).astype(jnp.float32)
    decayed = jnp.where(allowed[None], jnp.exp(-decay_rates[:, None, None] * spans[None]), 0.0)
    weights = (decayed * scores).astype(jnp.bfloat16)
    return jnp.einsum("hst,thf->shf", weights.astype(jnp.float32), grad_blk.astype(jnp.float32))


def state_terms(query_blk, grad_blk, decay_rates, doc_blk, pos_blk, doc_before, pos_before):
    spans = (pos_blk - pos_before).astype(jnp.float32)
    lead_decay = jnp.where((doc_blk == doc_before)[:, None], jnp.exp(-decay_rates[None, :] * spans[:, None]), 0.0)
    scaled = (query_blk.astype(jnp.float32) * lead_decay[:, :, None]).astype(jnp.bfloat16)
    local_state = jnp.einsum("the,thf->hef", scaled.astype(jnp.float32), grad_blk.astype(jnp.float32))
    whole_span = (pos_blk[-1] - pos_before).astype(jnp.float32)
    link_decay = jnp.where(doc_blk[-1] == doc_before, jnp.exp(-decay_rates * whole_span), 0.0)
    return local_state, link_decay


def inter_terms(key_blk, carried, decay_rates, doc_blk, pos_blk):
    spans = (pos_blk[-1] - pos_blk).astype(jnp.float32)
    tail_decay = jnp.where((doc_blk == doc_blk[-1])[:, None], jnp.exp(-decay_rates[None, :] * spans[:, None]), 0.0)
    rounded_state = carried.astype(jnp.bfloat16).astype(jnp.float32)
    product = jnp.einsum("she,hef->shf", key_blk.astype(jnp.float32), rounded_state) / HEAD_DIM
    return product * tail_decay[:, :, None]


def reference(queries, key_vectors, output_grad, value_weight, decay_rate, doc_lengths, owner_block, row_offset):
    block_count = TOKENS // TOK_DEV
    doc_ends = jnp.cumsum(doc_lengths).astype(jnp.int32)
    positions = jnp.arange(TOKENS, dtype=jnp.int32)
    doc_index = doc_of(positions, doc_ends)
    query_blocks = queries.reshape(block_count, TOK_DEV, HEADS, HEAD_DIM)
    key_blocks = key_vectors.reshape(block_count, TOK_DEV, HEADS, HEAD_DIM)
    grad_blocks = output_grad.reshape(block_count, TOK_DEV, HEADS, HEAD_DIM)
    pos_blocks = positions.reshape(block_count, TOK_DEV)
    doc_blocks = doc_index.reshape(block_count, TOK_DEV)

    def visit(carried, block_id):
        query_blk = query_blocks[block_id]
        key_blk = key_blocks[block_id]
        grad_blk = grad_blocks[block_id]
        pos_blk = pos_blocks[block_id]
        doc_blk = doc_blocks[block_id]
        pos_before = pos_blk[0] - 1
        doc_before = doc_of(jnp.maximum(pos_before, 0)[None], doc_ends)[0]
        intra_part = intra_terms(query_blk, key_blk, grad_blk, decay_rate, doc_blk, pos_blk)
        local_state, link_decay = state_terms(query_blk, grad_blk, decay_rate, doc_blk, pos_blk, doc_before, pos_before)
        inter_part = inter_terms(key_blk, carried, decay_rate, doc_blk, pos_blk)
        value_grad = (intra_part + inter_part).astype(jnp.bfloat16)
        carried_next = link_decay[:, None, None] * carried + local_state
        return carried_next, value_grad

    block_ids = jnp.arange(block_count - 1, -1, -1, dtype=jnp.int32)
    carried_init = jnp.zeros((HEADS, HEAD_DIM, HEAD_DIM), jnp.float32)
    final_state, grads_back = lax.scan(visit, carried_init, block_ids)
    value_grad = jnp.flip(grads_back, 0).reshape(TOKENS, HEADS * HEAD_DIM)

    group_width = HEADS * HEAD_DIM // N_HEAD
    token_grad = jnp.zeros((TOKENS, D), jnp.float32)
    for group_id in range(N_HEAD):
        low_col = group_id * group_width
        group_part = jnp.dot(value_grad[:, low_col:low_col + group_width], value_weight[:, low_col:low_col + group_width].T, preferred_element_type=jnp.float32)
        rounded = lax.optimization_barrier(group_part.astype(jnp.bfloat16))
        token_grad = token_grad + rounded.astype(jnp.float32)
    token_grad = lax.optimization_barrier(token_grad.astype(jnp.bfloat16)).astype(jnp.float32)

    owners = owner_block[:, 0].astype(jnp.int32)
    token_ids = owners * VROWS + row_offset.astype(jnp.int32)
    sort_order = jnp.argsort(token_ids, stable=True).astype(jnp.int32)
    sorted_ids = token_ids[sort_order]
    new_group = jnp.concatenate([jnp.zeros((1,), jnp.int32), (sorted_ids[1:] != sorted_ids[:-1]).astype(jnp.int32)])
    group_index = jnp.cumsum(new_group).astype(jnp.int32)
    group_sums = jax.ops.segment_sum(token_grad[sort_order], group_index, num_segments=TOKENS)
    row_total = jnp.zeros_like(token_grad).at[sort_order].set(group_sums[group_index])

    block_owners = owners.reshape(DEVICES, ROWS_BLK)
    same_owner = block_owners[:, :, None] == block_owners[:, None, :]
    lower_index = jnp.arange(ROWS_BLK, dtype=jnp.int32)
    earlier = lower_index[None, :] < lower_index[:, None]
    slot_rank = jnp.sum((same_owner & earlier[None]).astype(jnp.int32), axis=2).reshape(-1)
    block_of = (positions // ROWS_BLK).astype(jnp.int32)
    row_grads = jnp.zeros((DEVICES, DEVICES, CAP, D), jnp.bfloat16)
    row_grads = row_grads.at[owners, block_of, slot_rank].set(row_total.astype(jnp.bfloat16))
    return row_grads
```

```python
import jax
import jax.numpy as jnp
from jax import lax
from jax.sharding import PartitionSpec as P

def doc_of(positions, doc_ends):
    return jnp.sum((positions[:, None] >= doc_ends[None, :]).astype(jnp.int32), axis=1)


def intra_terms(query_blk, key_blk, grad_blk, decay_rates, doc_blk, pos_blk):
    head_dim = query_blk.shape[-1]
    scores = (
        jnp.einsum("she,the->hst", key_blk, query_blk, preferred_element_type=jnp.float32)
        / head_dim
    )
    distance = pos_blk[None, :] - pos_blk[:, None]
    allowed = (distance >= 0) & (doc_blk[:, None] == doc_blk[None, :])
    spans = jnp.maximum(distance, 0).astype(jnp.float32)
    decayed = jnp.where(allowed[None], jnp.exp(-decay_rates[:, None, None] * spans[None]), 0.0)
    weights = (decayed * scores).astype(jnp.bfloat16)
    return jnp.einsum("hst,thf->shf", weights, grad_blk, preferred_element_type=jnp.float32)


def state_terms(query_blk, grad_blk, decay_rates, doc_blk, pos_blk, doc_before, pos_before):
    spans = (pos_blk - pos_before).astype(jnp.float32)
    lead_decay = jnp.where(
        (doc_blk == doc_before)[:, None], jnp.exp(-decay_rates[None, :] * spans[:, None]), 0.0
    )
    scaled = (query_blk.astype(jnp.float32) * lead_decay[:, :, None]).astype(jnp.bfloat16)
    local_state = jnp.einsum("the,thf->hef", scaled, grad_blk, preferred_element_type=jnp.float32)
    whole_span = (pos_blk[-1] - pos_before).astype(jnp.float32)
    link_decay = jnp.where(doc_blk[-1] == doc_before, jnp.exp(-decay_rates * whole_span), 0.0)
    return (local_state, link_decay)


def inter_terms(key_blk, carried, decay_rates, doc_blk, pos_blk):
    head_dim = key_blk.shape[-1]
    spans = (pos_blk[-1] - pos_blk).astype(jnp.float32)
    tail_decay = jnp.where(
        (doc_blk == doc_blk[-1])[:, None], jnp.exp(-decay_rates[None, :] * spans[:, None]), 0.0
    )
    product = (
        jnp.einsum(
            "she,hef->shf",
            key_blk,
            carried.astype(jnp.bfloat16),
            preferred_element_type=jnp.float32,
        )
        / head_dim
    )
    return product * tail_decay[:, :, None]


def later_states(local_state, decay_rates, doc_ends, n_seq, tok_rows):
    heads, head_dim, width = local_state.shape
    piece = heads * head_dim // n_seq
    sent = local_state.reshape(n_seq, piece, width)
    got = lax.all_to_all(sent, "seq", split_axis=0, concat_axis=0, tiled=True)
    first = jnp.arange(n_seq, dtype=jnp.int32) * tok_rows
    doc_before = doc_of(jnp.maximum(first - 1, 0), doc_ends)
    doc_last = doc_of(first + tok_rows - 1, doc_ends)
    link = jnp.where(
        (doc_before == doc_last)[:, None], jnp.exp(-decay_rates * float(tok_rows))[None, :], 0.0
    )
    link_rows = jnp.repeat(link, head_dim, axis=1)
    mine = lax.dynamic_slice_in_dim(link_rows, lax.axis_index("seq") * piece, piece, axis=1)
    carried = jnp.zeros((piece, width), jnp.float32)
    states = [carried]
    for block in range(n_seq - 1, 0, -1):
        carried = mine[block][:, None] * carried + got[block]
        states.append(carried)
    back = jnp.stack(states[::-1]).astype(jnp.bfloat16)
    back = lax.all_to_all(back, "seq", split_axis=0, concat_axis=0, tiled=True)
    return back.reshape(heads, head_dim, width)


def slot_matrix(owners, capacity, owner_count):
    width = owners.shape[0]
    lower = jnp.arange(width, dtype=jnp.int32)
    same = (owners[:, None] == owners[None, :]) & (lower[None, :] < lower[:, None])
    slot = owners * capacity + jnp.sum(same.astype(jnp.int32), axis=1)
    slots = jnp.arange(owner_count * capacity, dtype=jnp.int32)
    return (slots[:, None] == slot[None, :]).astype(jnp.bfloat16)


def per_device(
    queries,
    key_vectors,
    output_grad,
    value_weight,
    decay_rate,
    doc_lengths,
    owner_block,
    row_offset,
):
    n_seq = lax.axis_size("seq")
    n_head = lax.axis_size("head")
    devices_all = n_seq * n_head
    n_hi = n_seq // 2
    tok_rows = queries.shape[0]
    head_local = decay_rate.shape[0]
    head_dim = queries.shape[1] // head_local
    seq_rank = lax.axis_index("seq")
    head_rank = lax.axis_index("head")
    block_rows = tok_rows // n_head
    capacity = max(2, 2 * block_rows // devices_all)
    swap = [(i, i ^ 1) for i in range(n_seq)]

    stride = [[2 * i + low for i in range(n_hi)] for low in range(2)]
    weights = lax.all_gather(
        value_weight, "seq", axis=0, tiled=True, axis_index_groups=stride
    )
    half = weights.shape[0]

    tags_own = jnp.stack([owner_block[:, 0], row_offset])
    tags_pair = lax.ppermute(tags_own, "seq", swap)

    first_row = seq_rank * tok_rows
    positions = first_row + jnp.arange(tok_rows, dtype=jnp.int32)
    doc_ends = jnp.cumsum(doc_lengths)
    doc_index = doc_of(positions, doc_ends)
    pos_before = first_row - 1
    doc_before = doc_of(jnp.maximum(pos_before, 0)[None], doc_ends)[0]
    query_blk = queries.reshape(tok_rows, head_local, head_dim)
    key_blk = key_vectors.reshape(tok_rows, head_local, head_dim)
    grad_blk = output_grad.reshape(tok_rows, head_local, head_dim)
    local_state, _ = state_terms(
        query_blk, grad_blk, decay_rate, doc_index, positions, doc_before, pos_before
    )
    carried = later_states(local_state, decay_rate, doc_ends, n_seq, tok_rows)
    intra_part = intra_terms(query_blk, key_blk, grad_blk, decay_rate, doc_index, positions)
    inter_part = inter_terms(key_blk, carried, decay_rate, doc_index, positions)
    value_own = (
        (intra_part + inter_part).astype(jnp.bfloat16).reshape(tok_rows, head_local * head_dim)
    )
    value_pair = lax.ppermute(value_own, "seq", swap)

    def routed(value_rows, tags):
        part = lax.dot_general(
            value_rows, weights, (((1,), (1,)), ((), ())), preferred_element_type=jnp.float32
        ).astype(jnp.bfloat16)
        parts = lax.all_to_all(
            part.reshape(n_head, block_rows, half), "head", split_axis=0, concat_axis=0, tiled=True
        )
        rows = jnp.sum(parts.astype(jnp.float32), axis=0).astype(jnp.bfloat16)
        mine = lax.dynamic_slice_in_dim(tags, head_rank * block_rows, block_rows, axis=1)
        offsets = mine[1]
        marks = jnp.stack([offsets // 64, offsets % 64, jnp.ones_like(offsets)], axis=1)
        marks = jnp.pad(marks.astype(jnp.bfloat16), ((0, 0), (0, 125)))
        places = slot_matrix(mine[0], capacity, devices_all)
        sent = jnp.dot(
            places, jnp.concatenate([rows, marks], axis=1), preferred_element_type=jnp.float32
        ).astype(jnp.bfloat16)
        got = lax.all_to_all(
            sent.reshape(devices_all, capacity, half + 128),
            ("seq", "head"),
            split_axis=0,
            concat_axis=0,
            tiled=True,
        )
        return got.reshape(n_hi, 2, n_head * capacity, half + 128)

    got_own = routed(value_own, tags_own)
    got_pair = routed(value_pair, tags_pair)

    def marks_of(got, low):
        return got[:, low, :, half:half + 3].astype(jnp.float32).reshape(-1, 3)

    seen = [marks_of(got_own, 0), marks_of(got_pair, 0)]
    keys = [jnp.where(m[:, 2] > 0, m[:, 0] * 64.0 + m[:, 1], -1.0) for m in seen]
    whole = jnp.stack([k.reshape(n_hi, -1) for k in keys], axis=1).reshape(-1)
    halves = []
    for low in range(2):
        total = 0.0
        for got, key in ((got_own, keys[low]), (got_pair, keys[1 - low])):
            equal = ((whole[:, None] == key[None, :]) & (whole >= 0)[:, None]).astype(jnp.bfloat16)
            data = got[:, low, :, :half].reshape(-1, half)
            total = total + jnp.dot(equal, data, preferred_element_type=jnp.float32)
        halves.append(total.astype(jnp.bfloat16).reshape(-1, n_hi, half // n_hi))
    row_grads = jnp.stack(halves, axis=2)
    return row_grads.reshape(1, devices_all, capacity, 2 * half)


def solution(mesh):
    return jax.shard_map(
        per_device,
        mesh=mesh,
        in_specs=(
            P("seq", "head"),
            P("seq", "head"),
            P("seq", "head"),
            P("seq", "head"),
            P("head"),
            P(),
            P("seq", None),
            P("seq"),
        ),
        out_specs=P(("seq", "head"), None, None, None),
        check_vma=False,
    )
```

```python
import jax
import jax.numpy as jnp
from jax import lax
from jax.experimental import pallas as pl
from jax.sharding import PartitionSpec as P

def doc_of(positions, doc_ends):
    return jnp.sum((positions[:, None] >= doc_ends[None, :]).astype(jnp.int32), axis=1)


def intra_terms(query_blk, key_blk, grad_blk, decay_rates, doc_blk, pos_blk):
    head_dim = query_blk.shape[-1]
    scores = (
        jnp.einsum("she,the->hst", key_blk, query_blk, preferred_element_type=jnp.float32)
        / head_dim
    )
    distance = pos_blk[None, :] - pos_blk[:, None]
    allowed = (distance >= 0) & (doc_blk[:, None] == doc_blk[None, :])
    spans = jnp.maximum(distance, 0).astype(jnp.float32)
    decayed = jnp.where(allowed[None], jnp.exp(-decay_rates[:, None, None] * spans[None]), 0.0)
    weights = (decayed * scores).astype(jnp.bfloat16)
    return jnp.einsum("hst,thf->shf", weights, grad_blk, preferred_element_type=jnp.float32)


def state_terms(query_blk, grad_blk, decay_rates, doc_blk, pos_blk, doc_before, pos_before):
    spans = (pos_blk - pos_before).astype(jnp.float32)
    lead_decay = jnp.where(
        (doc_blk == doc_before)[:, None], jnp.exp(-decay_rates[None, :] * spans[:, None]), 0.0
    )
    scaled = (query_blk.astype(jnp.float32) * lead_decay[:, :, None]).astype(jnp.bfloat16)
    local_state = jnp.einsum("the,thf->hef", scaled, grad_blk, preferred_element_type=jnp.float32)
    whole_span = (pos_blk[-1] - pos_before).astype(jnp.float32)
    link_decay = jnp.where(doc_blk[-1] == doc_before, jnp.exp(-decay_rates * whole_span), 0.0)
    return (local_state, link_decay)


def inter_terms(key_blk, carried, decay_rates, doc_blk, pos_blk):
    head_dim = key_blk.shape[-1]
    spans = (pos_blk[-1] - pos_blk).astype(jnp.float32)
    tail_decay = jnp.where(
        (doc_blk == doc_blk[-1])[:, None], jnp.exp(-decay_rates[None, :] * spans[:, None]), 0.0
    )
    product = (
        jnp.einsum(
            "she,hef->shf",
            key_blk,
            carried.astype(jnp.bfloat16),
            preferred_element_type=jnp.float32,
        )
        / head_dim
    )
    return product * tail_decay[:, :, None]


def later_states(local_state, decay_rates, doc_ends, n_seq, tok_rows):
    heads, head_dim, width = local_state.shape
    piece = heads * head_dim // n_seq
    sent = local_state.reshape(n_seq, piece, width)
    got = lax.all_to_all(sent, "seq", split_axis=0, concat_axis=0, tiled=True)
    first = jnp.arange(n_seq, dtype=jnp.int32) * tok_rows
    doc_before = doc_of(jnp.maximum(first - 1, 0), doc_ends)
    doc_last = doc_of(first + tok_rows - 1, doc_ends)
    link = jnp.where(
        (doc_before == doc_last)[:, None], jnp.exp(-decay_rates * float(tok_rows))[None, :], 0.0
    )
    link_rows = jnp.repeat(link, head_dim, axis=1)
    mine = lax.dynamic_slice_in_dim(link_rows, lax.axis_index("seq") * piece, piece, axis=1)
    carried = jnp.zeros((piece, width), jnp.float32)
    states = [carried]
    for block in range(n_seq - 1, 0, -1):
        carried = mine[block][:, None] * carried + got[block]
        states.append(carried)
    back = jnp.stack(states[::-1]).astype(jnp.bfloat16)
    back = lax.all_to_all(back, "seq", split_axis=0, concat_axis=0, tiled=True)
    return back.reshape(heads, head_dim, width)


def slot_matrix(owners, capacity, owner_count):
    width = owners.shape[0]
    lower = jnp.arange(width, dtype=jnp.int32)
    same = (owners[:, None] == owners[None, :]) & (lower[None, :] < lower[:, None])
    slot = owners * capacity + jnp.sum(same.astype(jnp.int32), axis=1)
    slots = jnp.arange(owner_count * capacity, dtype=jnp.int32)
    return (slots[:, None] == slot[None, :]).astype(jnp.bfloat16)


def head_sum(parts):
    n_head = lax.axis_size("head")
    head_rank = lax.axis_index("head")
    step = 1
    while step < n_head:
        bit = (head_rank // step) % 2
        pairs = parts.reshape((parts.shape[0] // 2, 2) + parts.shape[1:])
        sent = lax.dynamic_index_in_dim(pairs, 1 - bit, axis=1, keepdims=False)
        kept = lax.dynamic_index_in_dim(pairs, bit, axis=1, keepdims=False)
        got = lax.ppermute(sent, "head", [(i, i ^ step) for i in range(n_head)])
        parts = (kept.astype(jnp.float32) + got.astype(jnp.float32)).astype(jnp.bfloat16)
        step *= 2
    return parts[0]


def merge_kernel(equal_own, equal_pair, rows_own, rows_pair, out):
    shape = (-1, rows_own.shape[-1])
    total = jnp.dot(
        equal_own[0], rows_own[...].reshape(shape), preferred_element_type=jnp.float32
    )
    total += jnp.dot(
        equal_pair[0], rows_pair[...].reshape(shape), preferred_element_type=jnp.float32
    )
    out[...] = total.astype(out.dtype)


def merged(equal, got_own, got_pair, half):
    n_hi, _, rows, _ = got_own.shape
    width = half // n_hi
    slots = equal.shape[1]
    if width % 128 == 0 and rows % 16 == 0:
        matrix = (1, slots, equal.shape[2])
        data = pl.BlockSpec((n_hi, 1, rows, width), lambda i, low: (0, low, 0, i))
        return pl.pallas_call(
            merge_kernel,
            grid=(n_hi, 2),
            in_specs=[
                pl.BlockSpec(matrix, lambda i, low: (low, 0, 0)),
                pl.BlockSpec(matrix, lambda i, low: (1 - low, 0, 0)),
                data,
                data,
            ],
            out_specs=pl.BlockSpec((slots, width), lambda i, low: (0, 2 * i + low)),
            out_shape=jax.ShapeDtypeStruct((slots, 2 * half), jnp.bfloat16),
        )(equal, equal, got_own, got_pair)
    halves = []
    for low in range(2):
        total = 0.0
        for got, match in ((got_own, equal[low]), (got_pair, equal[1 - low])):
            data = got[:, low, :, :half].reshape(-1, half)
            total = total + jnp.dot(match, data, preferred_element_type=jnp.float32)
        halves.append(total.astype(jnp.bfloat16).reshape(-1, n_hi, width))
    return jnp.stack(halves, axis=2).reshape(slots, 2 * half)


def per_device(
    queries,
    key_vectors,
    output_grad,
    value_weight,
    decay_rate,
    doc_lengths,
    owner_block,
    row_offset,
):
    n_seq = lax.axis_size("seq")
    n_head = lax.axis_size("head")
    devices_all = n_seq * n_head
    n_hi = n_seq // 2
    tok_rows = queries.shape[0]
    head_local = decay_rate.shape[0]
    head_dim = queries.shape[1] // head_local
    seq_rank = lax.axis_index("seq")
    head_rank = lax.axis_index("head")
    block_rows = tok_rows // n_head
    capacity = max(2, 2 * block_rows // devices_all)
    swap = [(i, i ^ 1) for i in range(n_seq)]

    stride = [[2 * i + low for i in range(n_hi)] for low in range(2)]
    weights = lax.all_gather(
        value_weight, "seq", axis=0, tiled=True, axis_index_groups=stride
    )
    half = weights.shape[0]

    tags_own = jnp.stack([owner_block[:, 0], row_offset])
    tags_pair = lax.ppermute(tags_own, "seq", swap)

    first_row = seq_rank * tok_rows
    positions = first_row + jnp.arange(tok_rows, dtype=jnp.int32)
    doc_ends = jnp.cumsum(doc_lengths)
    doc_index = doc_of(positions, doc_ends)
    pos_before = first_row - 1
    doc_before = doc_of(jnp.maximum(pos_before, 0)[None], doc_ends)[0]
    query_blk = queries.reshape(tok_rows, head_local, head_dim)
    key_blk = key_vectors.reshape(tok_rows, head_local, head_dim)
    grad_blk = output_grad.reshape(tok_rows, head_local, head_dim)
    local_state, _ = state_terms(
        query_blk, grad_blk, decay_rate, doc_index, positions, doc_before, pos_before
    )
    carried = later_states(local_state, decay_rate, doc_ends, n_seq, tok_rows)
    intra_part = intra_terms(query_blk, key_blk, grad_blk, decay_rate, doc_index, positions)
    inter_part = inter_terms(key_blk, carried, decay_rate, doc_index, positions)
    value_own = (
        (intra_part + inter_part).astype(jnp.bfloat16).reshape(tok_rows, head_local * head_dim)
    )
    value_pair = lax.ppermute(value_own, "seq", swap)
    weights, value_pair = lax.optimization_barrier((weights, value_pair))

    def routed(value_rows, tags):
        part = lax.dot_general(
            value_rows, weights, (((1,), (1,)), ((), ())), preferred_element_type=jnp.float32
        ).astype(jnp.bfloat16)
        rows = head_sum(part.reshape(n_head, block_rows, half))
        mine = lax.dynamic_slice_in_dim(tags, head_rank * block_rows, block_rows, axis=1)
        offsets = mine[1]
        marks = jnp.stack([offsets // 64, offsets % 64, jnp.ones_like(offsets)], axis=1)
        marks = jnp.pad(marks.astype(jnp.bfloat16), ((0, 0), (0, 125)))
        places = slot_matrix(mine[0], capacity, devices_all)
        sent = jnp.dot(
            places, jnp.concatenate([rows, marks], axis=1), preferred_element_type=jnp.float32
        ).astype(jnp.bfloat16)
        got = lax.all_to_all(
            sent.reshape(devices_all, capacity, half + 128),
            ("seq", "head"),
            split_axis=0,
            concat_axis=0,
            tiled=True,
        )
        return got.reshape(n_hi, 2, n_head * capacity, half + 128)

    got_own = routed(value_own, tags_own)
    got_pair = routed(value_pair, tags_pair)

    def marks_of(got, low):
        return got[:, low, :, half:half + 3].astype(jnp.float32).reshape(-1, 3)

    seen = [marks_of(got_own, 0), marks_of(got_pair, 0)]
    keys = [jnp.where(m[:, 2] > 0, m[:, 0] * 64.0 + m[:, 1], -1.0) for m in seen]
    whole = jnp.stack([k.reshape(n_hi, -1) for k in keys], axis=1).reshape(-1)
    equal = jnp.stack([
        ((whole[:, None] == key[None, :]) & (whole >= 0)[:, None]).astype(jnp.bfloat16)
        for key in keys
    ])
    row_grads = merged(equal, got_own, got_pair, half)
    return row_grads.reshape(1, devices_all, capacity, 2 * half)


def solution(mesh):
    return jax.shard_map(
        per_device,
        mesh=mesh,
        in_specs=(
            P("seq", "head"),
            P("seq", "head"),
            P("seq", "head"),
            P("seq", "head"),
            P("head"),
            P(),
            P("seq", None),
            P("seq"),
        ),
        out_specs=P(("seq", "head"), None, None, None),
        check_vma=False,
    )
```

```python
import jax
import jax.numpy as jnp
from jax import lax
from jax.experimental import pallas as pl
from jax.sharding import PartitionSpec as P
QUADS = 4


def doc_of(positions, doc_ends):
    return jnp.sum((positions[:, None] >= doc_ends[None, :]).astype(jnp.int32), axis=1)


def intra_terms(query_blk, key_blk, grad_blk, decay_rates, doc_blk, pos_blk):
    head_dim = query_blk.shape[-1]
    scores = (
        jnp.einsum("she,the->hst", key_blk, query_blk, preferred_element_type=jnp.float32)
        / head_dim
    )
    distance = pos_blk[None, :] - pos_blk[:, None]
    allowed = (distance >= 0) & (doc_blk[:, None] == doc_blk[None, :])
    spans = jnp.maximum(distance, 0).astype(jnp.float32)
    decayed = jnp.where(allowed[None], jnp.exp(-decay_rates[:, None, None] * spans[None]), 0.0)
    weights = (decayed * scores).astype(jnp.bfloat16)
    return jnp.einsum("hst,thf->shf", weights, grad_blk, preferred_element_type=jnp.float32)


def state_terms(query_blk, grad_blk, decay_rates, doc_blk, pos_blk, doc_before, pos_before):
    spans = (pos_blk - pos_before).astype(jnp.float32)
    lead_decay = jnp.where(
        (doc_blk == doc_before)[:, None], jnp.exp(-decay_rates[None, :] * spans[:, None]), 0.0
    )
    scaled = (query_blk.astype(jnp.float32) * lead_decay[:, :, None]).astype(jnp.bfloat16)
    local_state = jnp.einsum("the,thf->hef", scaled, grad_blk, preferred_element_type=jnp.float32)
    whole_span = (pos_blk[-1] - pos_before).astype(jnp.float32)
    link_decay = jnp.where(doc_blk[-1] == doc_before, jnp.exp(-decay_rates * whole_span), 0.0)
    return (local_state, link_decay)


def inter_terms(key_blk, carried, decay_rates, doc_blk, pos_blk):
    head_dim = key_blk.shape[-1]
    spans = (pos_blk[-1] - pos_blk).astype(jnp.float32)
    tail_decay = jnp.where(
        (doc_blk == doc_blk[-1])[:, None], jnp.exp(-decay_rates[None, :] * spans[:, None]), 0.0
    )
    product = (
        jnp.einsum(
            "she,hef->shf",
            key_blk,
            carried.astype(jnp.bfloat16),
            preferred_element_type=jnp.float32,
        )
        / head_dim
    )
    return product * tail_decay[:, :, None]


def later_states(local_state, decay_rates, doc_ends, n_seq, tok_rows):
    heads, head_dim, width = local_state.shape
    piece = heads * head_dim // n_seq
    sent = local_state.reshape(n_seq, piece, width)
    got = lax.all_to_all(sent, "seq", split_axis=0, concat_axis=0, tiled=True)
    first = jnp.arange(n_seq, dtype=jnp.int32) * tok_rows
    doc_before = doc_of(jnp.maximum(first - 1, 0), doc_ends)
    doc_last = doc_of(first + tok_rows - 1, doc_ends)
    link = jnp.where(
        (doc_before == doc_last)[:, None], jnp.exp(-decay_rates * float(tok_rows))[None, :], 0.0
    )
    link_rows = jnp.repeat(link, head_dim, axis=1)
    mine = lax.dynamic_slice_in_dim(link_rows, lax.axis_index("seq") * piece, piece, axis=1)
    carried = jnp.zeros((piece, width), jnp.float32)
    states = [carried]
    for block in range(n_seq - 1, 0, -1):
        carried = mine[block][:, None] * carried + got[block]
        states.append(carried)
    back = jnp.stack(states[::-1]).astype(jnp.bfloat16)
    back = lax.all_to_all(back, "seq", split_axis=0, concat_axis=0, tiled=True)
    return back.reshape(heads, head_dim, width)


def slot_matrix(owners, capacity, owner_count):
    width = owners.shape[0]
    lower = jnp.arange(width, dtype=jnp.int32)
    same = (owners[:, None] == owners[None, :]) & (lower[None, :] < lower[:, None])
    slot = owners * capacity + jnp.sum(same.astype(jnp.int32), axis=1)
    slots = jnp.arange(owner_count * capacity, dtype=jnp.int32)
    return (slots[:, None] == slot[None, :]).astype(jnp.bfloat16)


def head_sum(parts):
    n_head = lax.axis_size("head")
    head_rank = lax.axis_index("head")
    step = 1
    while step < n_head:
        bit = (head_rank // step) % 2
        pairs = parts.reshape((parts.shape[0] // 2, 2) + parts.shape[1:])
        sent = lax.dynamic_index_in_dim(pairs, 1 - bit, axis=1, keepdims=False)
        kept = lax.dynamic_index_in_dim(pairs, bit, axis=1, keepdims=False)
        got = lax.ppermute(sent, "head", [(i, i ^ step) for i in range(n_head)])
        parts = (kept.astype(jnp.float32) + got.astype(jnp.float32)).astype(jnp.bfloat16)
        step *= 2
    return parts[0]


def merge_kernel(equal, *refs):
    data, out = refs[:-1], refs[-1]
    rows = jnp.concatenate([ref[...].reshape(-1, ref.shape[-1]) for ref in data], axis=0)
    total = jnp.dot(equal[0], rows, preferred_element_type=jnp.float32)
    out[...] = total.astype(out.dtype)


def merged(equal, got, part):
    n_hi, _, rows, _ = got[0].shape
    width = part // n_hi
    slots = equal.shape[1]
    if width % 128 == 0 and rows % 16 == 0:
        data = pl.BlockSpec((n_hi, 1, rows, width), lambda i, q: (0, q, 0, i))
        return pl.pallas_call(
            merge_kernel,
            grid=(n_hi, QUADS),
            in_specs=[pl.BlockSpec((1, slots, slots), lambda i, q: (q, 0, 0))] + [data] * QUADS,
            out_specs=pl.BlockSpec((slots, width), lambda i, q: (0, QUADS * i + q)),
            out_shape=jax.ShapeDtypeStruct((slots, QUADS * part), jnp.bfloat16),
        )(equal, *got)
    sets = []
    for q in range(QUADS):
        data = jnp.concatenate([g[:, q, :, :part].reshape(-1, part) for g in got], axis=0)
        total = jnp.dot(equal[q], data, preferred_element_type=jnp.float32)
        sets.append(total.astype(jnp.bfloat16).reshape(-1, n_hi, width))
    return jnp.stack(sets, axis=2).reshape(slots, QUADS * part)


def per_device(
    queries,
    key_vectors,
    output_grad,
    value_weight,
    decay_rate,
    doc_lengths,
    owner_block,
    row_offset,
):
    n_seq = lax.axis_size("seq")
    n_head = lax.axis_size("head")
    devices_all = n_seq * n_head
    n_hi = n_seq // QUADS
    tok_rows = queries.shape[0]
    head_local = decay_rate.shape[0]
    head_dim = queries.shape[1] // head_local
    seq_rank = lax.axis_index("seq")
    head_rank = lax.axis_index("head")
    block_rows = tok_rows // n_head
    capacity = max(2, 2 * block_rows // devices_all)

    def from_pair(array, k):
        return lax.ppermute(array, "seq", [(i, i ^ k) for i in range(n_seq)])

    if n_hi == 2:
        there = from_pair(value_weight, QUADS)
        is_low = seq_rank < QUADS
        pieces = [(value_weight, there), (there, value_weight)]
        weights = [jnp.where(is_low, a, b) for a, b in pieces]
    else:
        stride = [[QUADS * i + q for i in range(n_hi)] for q in range(QUADS)]
        weights = [
            lax.all_gather(value_weight, "seq", axis=0, tiled=True, axis_index_groups=stride)
        ]
    weights = jnp.concatenate(weights, axis=0)
    width = weights.shape[0]

    owners_own = owner_block[:, 0]
    owners = [owners_own] + [from_pair(owners_own, k) for k in range(1, QUADS)]

    first_row = seq_rank * tok_rows
    positions = first_row + jnp.arange(tok_rows, dtype=jnp.int32)
    doc_ends = jnp.cumsum(doc_lengths)
    doc_index = doc_of(positions, doc_ends)
    pos_before = first_row - 1
    doc_before = doc_of(jnp.maximum(pos_before, 0)[None], doc_ends)[0]
    query_blk = queries.reshape(tok_rows, head_local, head_dim)
    key_blk = key_vectors.reshape(tok_rows, head_local, head_dim)
    grad_blk = output_grad.reshape(tok_rows, head_local, head_dim)
    local_state, _ = state_terms(
        query_blk, grad_blk, decay_rate, doc_index, positions, doc_before, pos_before
    )
    carried = later_states(local_state, decay_rate, doc_ends, n_seq, tok_rows)
    intra_part = intra_terms(query_blk, key_blk, grad_blk, decay_rate, doc_index, positions)
    inter_part = inter_terms(key_blk, carried, decay_rate, doc_index, positions)
    value_own = (
        (intra_part + inter_part).astype(jnp.bfloat16).reshape(tok_rows, head_local * head_dim)
    )
    value_1 = from_pair(value_own, 1)
    value_2 = from_pair(value_own, 2)
    value_3 = from_pair(value_2, 1)

    def routed(k, value_rows):
        part = lax.dot_general(
            value_rows, weights, (((1,), (1,)), ((), ())), preferred_element_type=jnp.float32
        ).astype(jnp.bfloat16)
        rows = head_sum(part.reshape(n_head, block_rows, width))
        start = head_rank * block_rows
        places = slot_matrix(
            lax.dynamic_slice_in_dim(owners[k], start, block_rows), capacity, devices_all
        )
        if k == 0:
            offsets = lax.dynamic_slice_in_dim(row_offset, start, block_rows)
            marks = jnp.stack([offsets // 64, offsets % 64, jnp.ones_like(offsets)], axis=1)
            marks = jnp.pad(marks.astype(jnp.bfloat16), ((0, 0), (0, 125)))
            rows = jnp.concatenate([rows, marks], axis=1)
        sent = jnp.dot(places, rows, preferred_element_type=jnp.float32).astype(jnp.bfloat16)
        got = lax.all_to_all(
            sent.reshape(devices_all, capacity, rows.shape[1]),
            ("seq", "head"),
            split_axis=0,
            concat_axis=0,
            tiled=True,
        )
        return got.reshape(n_hi, QUADS, n_head * capacity, rows.shape[1])

    got = [routed(k, v) for k, v in enumerate((value_own, value_1, value_2, value_3))]
    marks = got[0][..., width:width + 3].astype(jnp.float32)
    keys = jnp.where(marks[..., 2] > 0, marks[..., 0] * 64.0 + marks[..., 1], -1.0)
    whole = keys.reshape(-1, 1)
    equal = jnp.stack([
        (
            (whole == jnp.concatenate([keys[:, q ^ k].reshape(-1) for k in range(QUADS)]))
            & (whole >= 0)
        ).astype(jnp.bfloat16)
        for q in range(QUADS)
    ])
    row_grads = merged(equal, got, width)
    return row_grads.reshape(1, devices_all, capacity, QUADS * width)


def solution(mesh):
    return jax.shard_map(
        per_device,
        mesh=mesh,
        in_specs=(
            P("seq", "head"),
            P("seq", "head"),
            P("seq", "head"),
            P("seq", "head"),
            P("head"),
            P(),
            P("seq", None),
            P("seq"),
        ),
        out_specs=P(("seq", "head"), None, None, None),
        check_vma=False,
    )
```

```python
import jax
import jax.numpy as jnp
from jax import lax
from jax.experimental import pallas as pl
from jax.sharding import PartitionSpec as P
QUADS = 4


def doc_of(positions, doc_ends):
    return jnp.sum((positions[:, None] >= doc_ends[None, :]).astype(jnp.int32), axis=1)


def intra_terms(query_blk, key_blk, grad_blk, decay_rates, doc_blk, pos_blk):
    head_dim = query_blk.shape[-1]
    scores = (
        jnp.einsum("she,the->hst", key_blk, query_blk, preferred_element_type=jnp.float32)
        / head_dim
    )
    distance = pos_blk[None, :] - pos_blk[:, None]
    allowed = (distance >= 0) & (doc_blk[:, None] == doc_blk[None, :])
    spans = jnp.maximum(distance, 0).astype(jnp.float32)
    decayed = jnp.where(allowed[None], jnp.exp(-decay_rates[:, None, None] * spans[None]), 0.0)
    weights = (decayed * scores).astype(jnp.bfloat16)
    return jnp.einsum("hst,thf->shf", weights, grad_blk, preferred_element_type=jnp.float32)


def state_terms(query_blk, grad_blk, decay_rates, doc_blk, pos_blk, doc_before, pos_before):
    spans = (pos_blk - pos_before).astype(jnp.float32)
    lead_decay = jnp.where(
        (doc_blk == doc_before)[:, None], jnp.exp(-decay_rates[None, :] * spans[:, None]), 0.0
    )
    scaled = (query_blk.astype(jnp.float32) * lead_decay[:, :, None]).astype(jnp.bfloat16)
    local_state = jnp.einsum("the,thf->hef", scaled, grad_blk, preferred_element_type=jnp.float32)
    whole_span = (pos_blk[-1] - pos_before).astype(jnp.float32)
    link_decay = jnp.where(doc_blk[-1] == doc_before, jnp.exp(-decay_rates * whole_span), 0.0)
    return (local_state, link_decay)


def inter_terms(key_blk, carried, decay_rates, doc_blk, pos_blk):
    head_dim = key_blk.shape[-1]
    spans = (pos_blk[-1] - pos_blk).astype(jnp.float32)
    tail_decay = jnp.where(
        (doc_blk == doc_blk[-1])[:, None], jnp.exp(-decay_rates[None, :] * spans[:, None]), 0.0
    )
    product = (
        jnp.einsum(
            "she,hef->shf",
            key_blk,
            carried.astype(jnp.bfloat16),
            preferred_element_type=jnp.float32,
        )
        / head_dim
    )
    return product * tail_decay[:, :, None]


def later_states(local_state, decay_rates, doc_ends, n_seq, tok_rows):
    heads, head_dim, width = local_state.shape
    piece = heads * head_dim // n_seq
    sent = local_state.reshape(n_seq, piece, width)
    got = lax.all_to_all(sent, "seq", split_axis=0, concat_axis=0, tiled=True)
    first = jnp.arange(n_seq, dtype=jnp.int32) * tok_rows
    doc_before = doc_of(jnp.maximum(first - 1, 0), doc_ends)
    doc_last = doc_of(first + tok_rows - 1, doc_ends)
    link = jnp.where(
        (doc_before == doc_last)[:, None], jnp.exp(-decay_rates * float(tok_rows))[None, :], 0.0
    )
    link_rows = jnp.repeat(link, head_dim, axis=1)
    mine = lax.dynamic_slice_in_dim(link_rows, lax.axis_index("seq") * piece, piece, axis=1)
    carried = jnp.zeros((piece, width), jnp.float32)
    states = [carried]
    for block in range(n_seq - 1, 0, -1):
        carried = mine[block][:, None] * carried + got[block]
        states.append(carried)
    back = jnp.stack(states[::-1]).astype(jnp.bfloat16)
    back = lax.all_to_all(back, "seq", split_axis=0, concat_axis=0, tiled=True)
    return back.reshape(heads, head_dim, width)


def slot_matrix(owners, capacity, owner_count):
    width = owners.shape[0]
    lower = jnp.arange(width, dtype=jnp.int32)
    same = (owners[:, None] == owners[None, :]) & (lower[None, :] < lower[:, None])
    slot = owners * capacity + jnp.sum(same.astype(jnp.int32), axis=1)
    slots = jnp.arange(owner_count * capacity, dtype=jnp.int32)
    return (slots[:, None] == slot[None, :]).astype(jnp.bfloat16)


def head_sum(parts):
    n_head = lax.axis_size("head")
    head_rank = lax.axis_index("head")
    step = 1
    while step < n_head:
        bit = (head_rank // step) % 2
        pairs = parts.reshape((parts.shape[0] // 2, 2) + parts.shape[1:])
        sent = lax.dynamic_index_in_dim(pairs, 1 - bit, axis=1, keepdims=False)
        kept = lax.dynamic_index_in_dim(pairs, bit, axis=1, keepdims=False)
        got = lax.ppermute(sent, "head", [(i, i ^ step) for i in range(n_head)])
        parts = (kept.astype(jnp.float32) + got.astype(jnp.float32)).astype(jnp.bfloat16)
        step *= 2
    return parts[0]


def merge_kernel(equal, *refs):
    data, out = refs[:-1], refs[-1]
    rows = jnp.concatenate([ref[...].reshape(-1, ref.shape[-1]) for ref in data], axis=0)
    total = jnp.dot(equal[0], rows, preferred_element_type=jnp.float32)
    out[...] = total.astype(out.dtype)


def merged(equal, got, part):
    _, n_mid, _, rows, _ = got[0].shape
    width = part // n_mid
    slots = equal.shape[1]
    if width % 128 == 0 and rows % 16 == 0:
        data = pl.BlockSpec((1, n_mid, 1, rows, width), lambda t, i, u: (t, 0, u, 0, i))
        return pl.pallas_call(
            merge_kernel,
            grid=(2, n_mid, 2),
            in_specs=[pl.BlockSpec((1, slots, slots), lambda t, i, u: (2 * t + u, 0, 0))]
            + [data] * QUADS,
            out_specs=pl.BlockSpec(
                (slots, width), lambda t, i, u: (0, (t * n_mid + i) * 2 + u)
            ),
            out_shape=jax.ShapeDtypeStruct((slots, QUADS * part), jnp.bfloat16),
        )(equal, *got)
    sets = []
    for t in range(2):
        for u in range(2):
            data = jnp.concatenate([g[t, :, u, :, :part].reshape(-1, part) for g in got], axis=0)
            total = jnp.dot(equal[2 * t + u], data, preferred_element_type=jnp.float32)
            sets.append(total.astype(jnp.bfloat16).reshape(-1, n_mid, width))
    sides = [jnp.stack(sets[2 * t:2 * t + 2], axis=2) for t in range(2)]
    return jnp.stack(sides, axis=1).reshape(slots, QUADS * part)


def per_device(
    queries,
    key_vectors,
    output_grad,
    value_weight,
    decay_rate,
    doc_lengths,
    owner_block,
    row_offset,
):
    n_seq = lax.axis_size("seq")
    n_head = lax.axis_size("head")
    devices_all = n_seq * n_head
    n_mid = n_seq // QUADS
    top = n_seq // 2
    tok_rows = queries.shape[0]
    head_local = decay_rate.shape[0]
    head_dim = queries.shape[1] // head_local
    seq_rank = lax.axis_index("seq")
    head_rank = lax.axis_index("head")
    block_rows = tok_rows // n_head
    capacity = max(2, 2 * block_rows // devices_all)

    def from_pair(array, k):
        return lax.ppermute(array, "seq", [(i, i ^ k) for i in range(n_seq)])

    if n_mid == 2:
        there = from_pair(value_weight, 2)
        is_low = (seq_rank // 2) % 2 == 0
        pieces = [(value_weight, there), (there, value_weight)]
        weights = [jnp.where(is_low, a, b) for a, b in pieces]
    else:
        groups = [[t * top + 2 * m + u for m in range(n_mid)] for t in range(2) for u in range(2)]
        weights = [
            lax.all_gather(value_weight, "seq", axis=0, tiled=True, axis_index_groups=groups)
        ]
    weights = jnp.concatenate(weights, axis=0)
    width = weights.shape[0]

    owners_own = owner_block[:, 0]
    owners = [owners_own] + [from_pair(owners_own, k) for k in (1, top, top + 1)]

    first_row = seq_rank * tok_rows
    positions = first_row + jnp.arange(tok_rows, dtype=jnp.int32)
    doc_ends = jnp.cumsum(doc_lengths)
    doc_index = doc_of(positions, doc_ends)
    pos_before = first_row - 1
    doc_before = doc_of(jnp.maximum(pos_before, 0)[None], doc_ends)[0]
    query_blk = queries.reshape(tok_rows, head_local, head_dim)
    key_blk = key_vectors.reshape(tok_rows, head_local, head_dim)
    grad_blk = output_grad.reshape(tok_rows, head_local, head_dim)
    local_state, _ = state_terms(
        query_blk, grad_blk, decay_rate, doc_index, positions, doc_before, pos_before
    )
    carried = later_states(local_state, decay_rate, doc_ends, n_seq, tok_rows)
    intra_part = intra_terms(query_blk, key_blk, grad_blk, decay_rate, doc_index, positions)
    inter_part = inter_terms(key_blk, carried, decay_rate, doc_index, positions)
    value_own = (
        (intra_part + inter_part).astype(jnp.bfloat16).reshape(tok_rows, head_local * head_dim)
    )
    value_u = from_pair(value_own, 1)
    value_t = from_pair(value_own, top)
    value_tu = from_pair(value_t, 1)

    def reduced(value_rows):
        part = lax.dot_general(
            value_rows, weights, (((1,), (1,)), ((), ())), preferred_element_type=jnp.float32
        ).astype(jnp.bfloat16)
        return head_sum(part.reshape(n_head, block_rows, width))

    def routed(k, rows):
        start = head_rank * block_rows
        places = slot_matrix(
            lax.dynamic_slice_in_dim(owners[k], start, block_rows), capacity, devices_all
        )
        if k == 0:
            offsets = lax.dynamic_slice_in_dim(row_offset, start, block_rows)
            marks = jnp.stack([offsets // 64, offsets % 64, jnp.ones_like(offsets)], axis=1)
            marks = jnp.pad(marks.astype(jnp.bfloat16), ((0, 0), (0, 125)))
            rows = jnp.concatenate([rows, marks], axis=1)
        sent = jnp.dot(places, rows, preferred_element_type=jnp.float32).astype(jnp.bfloat16)
        got = lax.all_to_all(
            sent.reshape(devices_all, capacity, rows.shape[1]),
            ("seq", "head"),
            split_axis=0,
            concat_axis=0,
            tiled=True,
        )
        return got.reshape(2, n_mid, 2, n_head * capacity, rows.shape[1])

    rows_own = reduced(value_own)
    value_u, _ = lax.optimization_barrier((value_u, rows_own))
    got = [routed(0, rows_own)]
    for k, value_rows in enumerate((value_u, value_t, value_tu)):
        got.append(routed(k + 1, reduced(value_rows)))
    marks = got[0][..., width:width + 3].astype(jnp.float32)
    keys = jnp.where(marks[..., 2] > 0, marks[..., 0] * 64.0 + marks[..., 1], -1.0)
    whole = keys.reshape(-1, 1)
    equal = jnp.stack([
        (
            (whole == jnp.concatenate(
                [keys[t ^ a, :, u ^ b].reshape(-1) for a in range(2) for b in range(2)]
            ))
            & (whole >= 0)
        ).astype(jnp.bfloat16)
        for t in range(2)
        for u in range(2)
    ])
    row_grads = merged(equal, got, width)
    return row_grads.reshape(1, devices_all, capacity, QUADS * width)


def solution(mesh):
    return jax.shard_map(
        per_device,
        mesh=mesh,
        in_specs=(
            P("seq", "head"),
            P("seq", "head"),
            P("seq", "head"),
            P("seq", "head"),
            P("head"),
            P(),
            P("seq", None),
            P("seq"),
        ),
        out_specs=P(("seq", "head"), None, None, None),
        check_vma=False,
    )
```

```python
import jax
import jax.numpy as jnp
from jax import lax
from jax.experimental import pallas as pl
from jax.sharding import PartitionSpec as P
QUADS = 4


def doc_of(positions, doc_ends):
    return jnp.sum((positions[:, None] >= doc_ends[None, :]).astype(jnp.int32), axis=1)


def intra_terms(query_blk, key_blk, grad_blk, decay_rates, doc_blk, pos_blk):
    head_dim = query_blk.shape[-1]
    scores = (
        jnp.einsum("she,the->hst", key_blk, query_blk, preferred_element_type=jnp.float32)
        / head_dim
    )
    distance = pos_blk[None, :] - pos_blk[:, None]
    allowed = (distance >= 0) & (doc_blk[:, None] == doc_blk[None, :])
    spans = jnp.maximum(distance, 0).astype(jnp.float32)
    decayed = jnp.where(allowed[None], jnp.exp(-decay_rates[:, None, None] * spans[None]), 0.0)
    weights = (decayed * scores).astype(jnp.bfloat16)
    return jnp.einsum("hst,thf->shf", weights, grad_blk, preferred_element_type=jnp.float32)


def state_terms(query_blk, grad_blk, decay_rates, doc_blk, pos_blk, doc_before, pos_before):
    spans = (pos_blk - pos_before).astype(jnp.float32)
    lead_decay = jnp.where(
        (doc_blk == doc_before)[:, None], jnp.exp(-decay_rates[None, :] * spans[:, None]), 0.0
    )
    scaled = (query_blk.astype(jnp.float32) * lead_decay[:, :, None]).astype(jnp.bfloat16)
    local_state = jnp.einsum("the,thf->hef", scaled, grad_blk, preferred_element_type=jnp.float32)
    whole_span = (pos_blk[-1] - pos_before).astype(jnp.float32)
    link_decay = jnp.where(doc_blk[-1] == doc_before, jnp.exp(-decay_rates * whole_span), 0.0)
    return (local_state, link_decay)


def inter_terms(key_blk, carried, decay_rates, doc_blk, pos_blk):
    head_dim = key_blk.shape[-1]
    spans = (pos_blk[-1] - pos_blk).astype(jnp.float32)
    tail_decay = jnp.where(
        (doc_blk == doc_blk[-1])[:, None], jnp.exp(-decay_rates[None, :] * spans[:, None]), 0.0
    )
    product = (
        jnp.einsum(
            "she,hef->shf",
            key_blk,
            carried.astype(jnp.bfloat16),
            preferred_element_type=jnp.float32,
        )
        / head_dim
    )
    return product * tail_decay[:, :, None]


def later_states(local_state, decay_rates, doc_ends, n_seq, tok_rows):
    heads, head_dim, width = local_state.shape
    piece = heads * head_dim // n_seq
    sent = local_state.reshape(n_seq, piece, width)
    got = lax.all_to_all(sent, "seq", split_axis=0, concat_axis=0, tiled=True)
    first = jnp.arange(n_seq, dtype=jnp.int32) * tok_rows
    doc_before = doc_of(jnp.maximum(first - 1, 0), doc_ends)
    doc_last = doc_of(first + tok_rows - 1, doc_ends)
    link = jnp.where(
        (doc_before == doc_last)[:, None], jnp.exp(-decay_rates * float(tok_rows))[None, :], 0.0
    )
    link_rows = jnp.repeat(link, head_dim, axis=1)
    mine = lax.dynamic_slice_in_dim(link_rows, lax.axis_index("seq") * piece, piece, axis=1)
    carried = jnp.zeros((piece, width), jnp.float32)
    states = [carried]
    for block in range(n_seq - 1, 0, -1):
        carried = mine[block][:, None] * carried + got[block]
        states.append(carried)
    back = jnp.stack(states[::-1]).astype(jnp.bfloat16)
    back = lax.all_to_all(back, "seq", split_axis=0, concat_axis=0, tiled=True)
    return back.reshape(heads, head_dim, width)


def slot_matrix(owners, capacity, owner_count):
    width = owners.shape[0]
    lower = jnp.arange(width, dtype=jnp.int32)
    same = (owners[:, None] == owners[None, :]) & (lower[None, :] < lower[:, None])
    slot = owners * capacity + jnp.sum(same.astype(jnp.int32), axis=1)
    slots = jnp.arange(owner_count * capacity, dtype=jnp.int32)
    return (slots[:, None] == slot[None, :]).astype(jnp.bfloat16)


def head_sum(parts):
    n_head = lax.axis_size("head")
    head_rank = lax.axis_index("head")
    step = 1
    while step < n_head:
        bit = (head_rank // step) % 2
        pairs = parts.reshape((parts.shape[0] // 2, 2) + parts.shape[1:])
        sent = lax.dynamic_index_in_dim(pairs, 1 - bit, axis=1, keepdims=False)
        kept = lax.dynamic_index_in_dim(pairs, bit, axis=1, keepdims=False)
        got = lax.ppermute(sent, "head", [(i, i ^ step) for i in range(n_head)])
        parts = (kept.astype(jnp.float32) + got.astype(jnp.float32)).astype(jnp.bfloat16)
        step *= 2
    return parts[0]


def merge_kernel(equal, *refs):
    data, out = refs[:-1], refs[-1]
    rows = jnp.concatenate([ref[...].reshape(-1, ref.shape[-1]) for ref in data], axis=0)
    total = jnp.dot(equal[0], rows, preferred_element_type=jnp.float32)
    out[...] = total.astype(out.dtype)


def merged(equal, got, part):
    _, n_mid, _, rows, _ = got[0].shape
    width = part // n_mid
    slots = equal.shape[1]
    if width % 128 == 0 and rows % 16 == 0:
        data = pl.BlockSpec((1, n_mid, 1, rows, width), lambda t, i, u: (t, 0, u, 0, i))
        return pl.pallas_call(
            merge_kernel,
            grid=(2, n_mid, 2),
            in_specs=[pl.BlockSpec((1, slots, slots), lambda t, i, u: (2 * t + u, 0, 0))]
            + [data] * QUADS,
            out_specs=pl.BlockSpec(
                (slots, width), lambda t, i, u: (0, (t * n_mid + i) * 2 + u)
            ),
            out_shape=jax.ShapeDtypeStruct((slots, QUADS * part), jnp.bfloat16),
        )(equal, *got)
    sets = []
    for t in range(2):
        for u in range(2):
            data = jnp.concatenate([g[t, :, u, :, :part].reshape(-1, part) for g in got], axis=0)
            total = jnp.dot(equal[2 * t + u], data, preferred_element_type=jnp.float32)
            sets.append(total.astype(jnp.bfloat16).reshape(-1, n_mid, width))
    sides = [jnp.stack(sets[2 * t:2 * t + 2], axis=2) for t in range(2)]
    return jnp.stack(sides, axis=1).reshape(slots, QUADS * part)


def per_device(
    queries,
    key_vectors,
    output_grad,
    value_weight,
    decay_rate,
    doc_lengths,
    owner_block,
    row_offset,
):
    n_seq = lax.axis_size("seq")
    n_head = lax.axis_size("head")
    devices_all = n_seq * n_head
    n_mid = n_seq // QUADS
    top = n_seq // 2
    tok_rows = queries.shape[0]
    head_local = decay_rate.shape[0]
    head_dim = queries.shape[1] // head_local
    seq_rank = lax.axis_index("seq")
    head_rank = lax.axis_index("head")
    block_rows = tok_rows // n_head
    capacity = max(2, 2 * block_rows // devices_all)

    def from_pair(array, k):
        return lax.ppermute(array, "seq", [(i, i ^ k) for i in range(n_seq)])

    if n_mid == 2:
        there = from_pair(value_weight, 2)
        is_low = (seq_rank // 2) % 2 == 0
        pieces = [(value_weight, there), (there, value_weight)]
        weights = [jnp.where(is_low, a, b) for a, b in pieces]
    else:
        groups = [[t * top + 2 * m + u for m in range(n_mid)] for t in range(2) for u in range(2)]
        weights = [
            lax.all_gather(value_weight, "seq", axis=0, tiled=True, axis_index_groups=groups)
        ]
    weights = jnp.concatenate(weights, axis=0)
    width = weights.shape[0]

    owners_own = owner_block[:, 0]
    owners = [owners_own] + [from_pair(owners_own, k) for k in (1, top, top + 1)]

    first_row = seq_rank * tok_rows
    positions = first_row + jnp.arange(tok_rows, dtype=jnp.int32)
    doc_ends = jnp.cumsum(doc_lengths)
    doc_index = doc_of(positions, doc_ends)
    pos_before = first_row - 1
    doc_before = doc_of(jnp.maximum(pos_before, 0)[None], doc_ends)[0]
    query_blk = queries.reshape(tok_rows, head_local, head_dim)
    key_blk = key_vectors.reshape(tok_rows, head_local, head_dim)
    grad_blk = output_grad.reshape(tok_rows, head_local, head_dim)
    local_state, _ = state_terms(
        query_blk, grad_blk, decay_rate, doc_index, positions, doc_before, pos_before
    )
    carried = later_states(local_state, decay_rate, doc_ends, n_seq, tok_rows)
    intra_part = intra_terms(query_blk, key_blk, grad_blk, decay_rate, doc_index, positions)
    inter_part = inter_terms(key_blk, carried, decay_rate, doc_index, positions)
    value_own = (
        (intra_part + inter_part).astype(jnp.bfloat16).reshape(tok_rows, head_local * head_dim)
    )
    value_u = from_pair(value_own, 1)
    value_t = from_pair(value_own, top)

    def reduced(value_rows):
        part = lax.dot_general(
            value_rows, weights, (((1,), (1,)), ((), ())), preferred_element_type=jnp.float32
        ).astype(jnp.bfloat16)
        return head_sum(part.reshape(n_head, block_rows, width))

    def routed(k, rows):
        start = head_rank * block_rows
        places = slot_matrix(
            lax.dynamic_slice_in_dim(owners[k], start, block_rows), capacity, devices_all
        )
        if k == 0:
            offsets = lax.dynamic_slice_in_dim(row_offset, start, block_rows)
            marks = jnp.stack([offsets // 64, offsets % 64, jnp.ones_like(offsets)], axis=1)
            marks = jnp.pad(marks.astype(jnp.bfloat16), ((0, 0), (0, 125)))
            rows = jnp.concatenate([rows, marks], axis=1)
        sent = jnp.dot(places, rows, preferred_element_type=jnp.float32).astype(jnp.bfloat16)
        got = lax.all_to_all(
            sent.reshape(devices_all, capacity, rows.shape[1]),
            ("seq", "head"),
            split_axis=0,
            concat_axis=0,
            tiled=True,
        )
        return got.reshape(2, n_mid, 2, n_head * capacity, rows.shape[1])

    rows_own = reduced(value_own)
    value_u, _ = lax.optimization_barrier((value_u, rows_own))
    rows_u = reduced(value_u)
    value_t, _ = lax.optimization_barrier((value_t, rows_u))
    value_tu = from_pair(value_t, 1)
    got = [routed(0, rows_own), routed(1, rows_u)]
    for k, value_rows in enumerate((value_t, value_tu)):
        got.append(routed(k + 2, reduced(value_rows)))
    marks = got[0][..., width:width + 3].astype(jnp.float32)
    keys = jnp.where(marks[..., 2] > 0, marks[..., 0] * 64.0 + marks[..., 1], -1.0)
    whole = keys.reshape(-1, 1)
    equal = jnp.stack([
        (
            (whole == jnp.concatenate(
                [keys[t ^ a, :, u ^ b].reshape(-1) for a in range(2) for b in range(2)]
            ))
            & (whole >= 0)
        ).astype(jnp.bfloat16)
        for t in range(2)
        for u in range(2)
    ])
    row_grads = merged(equal, got, width)
    return row_grads.reshape(1, devices_all, capacity, QUADS * width)


def solution(mesh):
    return jax.shard_map(
        per_device,
        mesh=mesh,
        in_specs=(
            P("seq", "head"),
            P("seq", "head"),
            P("seq", "head"),
            P("seq", "head"),
            P("head"),
            P(),
            P("seq", None),
            P("seq"),
        ),
        out_specs=P(("seq", "head"), None, None, None),
        check_vma=False,
    )
```
